32 devices in a mesh: groups: 2 (over y), ctx: 4 (over z), head: 4 (over x, core).
Axes of the slice: x: 2, y: 2, z: 4, core: 2. Of those that a mesh axis runs over, the one named last changes fastest.
Arguments:
- query_rows: bfloat16 [4096, 4096], P(('groups', 'ctx', 'head')), parts along dimension 0, may hold values from -6 to 6
- key_rows: bfloat16 [4096, 4096], P(('groups', 'ctx', 'head')), parts along dimension 0, may hold values from -6 to 6
- value_rows: bfloat16 [4096, 8192], P(('groups', 'ctx', 'head')), parts along dimension 0, may hold values from -30 to 30
- gate_rows: bfloat16 [4096, 8192], P(('groups', 'ctx', 'head')), parts along dimension 0, may hold values from -6 to 6
- decay_log: bfloat16 [4096, 16], P(('groups', 'ctx', 'head')), parts along dimension 0, may hold values from -1 to 0, as said below
- norm_gain: float32 [8192], P('head'), may hold values from 0.25 to 1.75
Outputs:
- retention_out: bfloat16 [4096, 8192], P(('groups', 'ctx', 'head')), parts along dimension 0
The draws below stay inside these ranges and needn't reach their ends.
There are 2 independent parts, one for each index of `groups`. The reference program is written for one: setup_inputs(seed, part) draws one part's arguments, and reference() takes and returns one part's arrays. A program takes and returns all parts, laid end to end along the dimension named above; an argument that names none is the same for every part. Nothing has to cross between parts.
Inputs may be any that keep to these rules, and one draw needn't show every extreme that they name: `decay_log`: every entry is negative.
All inputs are finite; a program needn't handle non-finite values.
Results may differ from the reference program's by a relative error of at most 0.0085.
Values may be sent and summed in bfloat16 or wider, within the bound.
A program may use at most 128 MiB of HBM per device.

```python
import math
import jax
import jax.numpy as jnp
from jax import lax

HEADS = 16
KEY_DIM = 256
VALUE_DIM = 512
TOK_DEV = 128
BLOCK = 512
BLOCKS = 4
SEQ = 2048


def draw_decay_log(key, part):
    streams = jax.random.split(jax.random.fold_in(key, 11), 7)
    share = 0.5
    picked = jax.random.uniform(streams[0], (HEADS,))
    slow_rate = jnp.exp(jax.random.uniform(streams[1], (HEADS,), minval=math.log(0.1), maxval=math.log(0.6))) / SEQ
    fast_rate = jnp.exp(jax.random.uniform(streams[2], (HEADS,), minval=math.log(1.0 / 50.0), maxval=math.log(1.0 / 30.0)))
    rate = jnp.where(picked < share, fast_rate, slow_rate)
    spans = SEQ // TOK_DEV
    factor = jnp.exp(jax.random.uniform(streams[3], (spans, 1), minval=math.log(0.5), maxval=math.log(2.0)))
    factor = jnp.repeat(factor, TOK_DEV, axis=0)
    rough = jax.random.uniform(streams[4], (SEQ, HEADS), minval=0.6, maxval=1.4)
    spots = jax.random.randint(streams[5], (3,), 0, SEQ)
    bursty = jnp.any(jnp.arange(SEQ)[:, None] == spots[None, :], axis=1)
    losses = jax.random.uniform(streams[6], (SEQ, HEADS), minval=math.log(0.5), maxval=math.log(0.8))
    result = -rate[None, :] * factor * rough + jnp.where(bursty[:, None], losses, 0.0)
    return result.astype(jnp.bfloat16)


def draw_value_rows(key, part):
    streams = jax.random.split(jax.random.fold_in(key, 23), 3)
    width = HEADS * VALUE_DIM
    column_scale = jnp.exp(jax.random.uniform(streams[0], (1, width), minval=0.0, maxval=math.log(10.0)))
    row_scale = jnp.exp(jax.random.uniform(streams[1], (SEQ, 1), minval=0.0, maxval=math.log(10.0)))
    basis = jnp.clip(jax.random.normal(streams[2], (SEQ, width)), -3.0, 3.0)
    return (basis * column_scale * row_scale / 10.0).astype(jnp.bfloat16)


def steps_of(own_key, shape, pieces, least, largest):
    def one(position, parts):
        draws = jax.random.uniform(jax.random.fold_in(jax.random.fold_in(own_key, 6), position), (parts,), jnp.float32, least / len(pieces), largest / len(pieces))
        return jnp.repeat(jnp.exp(draws), shape[position] // parts).reshape((-1,) + (1,) * (len(shape) - position - 1))

    level = one(*pieces[0])
    for cut in pieces[1:]:
        level = level * one(*cut)
    return level


def centred(key, shape, deviation, bound, cuts=(), kind=jnp.bfloat16):
    array = deviation * jax.random.normal(key, shape, jnp.float32)
    if cuts:
        array = array * steps_of(key, shape, cuts, -0.22, 0.18)
    return jnp.clip(array, -bound, bound).astype(kind)


def setup_inputs(seed: int = 0, part: int = 0) -> dict:
    seeds = jax.random.split(jax.random.key(seed), 7)
    part_keys = jax.random.split(jax.random.fold_in(seeds[6], part), 7)
    return {
        "query_rows": centred(part_keys[0], (SEQ, HEADS * KEY_DIM), 1.0, 6.0, ((0, 16),)),
        "key_rows": centred(part_keys[1], (SEQ, HEADS * KEY_DIM), 1.0, 6.0, ((0, 16),)),
        "value_rows": draw_value_rows(jax.random.fold_in(jax.random.fold_in(seeds[6], part), 71), part),
        "gate_rows": centred(part_keys[3], (SEQ, HEADS * VALUE_DIM), 1.0, 6.0, ((0, 16),)),
        "decay_log": draw_decay_log(jax.random.fold_in(jax.random.fold_in(seeds[6], part), 71), part),
        "norm_gain": jnp.clip(1.0 + 0.15 * jax.random.normal(seeds[5], (HEADS * VALUE_DIM,), jnp.float32), 0.25, 1.75),
    }


def block_step(carried, inputs):
    query_block, key_block, value_block, decay_block = inputs
    length = query_block.shape[0]
    key_scale = KEY_DIM ** (-0.5)
    within = jnp.cumsum(decay_block.astype(jnp.float32), axis=0)
    block_total = within[-1]
    log_gaps = within.T[:, :, None] - within.T[:, None, :]
    causal = (jnp.arange(length)[:, None] >= jnp.arange(length)[None, :])[None]
    damping = jnp.where(causal, jnp.exp(jnp.where(causal, log_gaps, 0.0)), 0.0)
    query_wide = query_block.astype(jnp.float32)
    scores = jnp.einsum('ihk,jhk->hij', query_wide, key_block.astype(jnp.float32))
    weights = (scores * key_scale * damping).astype(jnp.bfloat16)
    local_out = jnp.einsum('hij,jhd->ihd', weights.astype(jnp.float32), value_block.astype(jnp.float32))
    decayed = (key_block.astype(jnp.float32) * jnp.exp(block_total[None, :] - within)[:, :, None]).astype(jnp.bfloat16)
    block_state = jnp.einsum('jhk,jhd->hkd', decayed.astype(jnp.float32), value_block.astype(jnp.float32))
    inter = jnp.einsum('ihk,hkd->ihd', query_wide, carried, precision=lax.Precision.HIGHEST)
    retained = local_out + inter * (jnp.exp(within) * key_scale)[:, :, None]
    updated = jnp.exp(block_total)[:, None, None] * carried + block_state
    return (updated, retained)

def reference(query_rows, key_rows, value_rows, gate_rows, decay_log, norm_gain):
    query_blocks = query_rows.reshape(BLOCKS, BLOCK, HEADS, KEY_DIM)
    key_blocks = key_rows.reshape(BLOCKS, BLOCK, HEADS, KEY_DIM)
    value_blocks = value_rows.reshape(BLOCKS, BLOCK, HEADS, VALUE_DIM)
    decay_blocks = decay_log.reshape(BLOCKS, BLOCK, HEADS)
    start_state = jnp.zeros((HEADS, KEY_DIM, VALUE_DIM), jnp.float32)
    final_state, retained = lax.scan(block_step, start_state, (query_blocks, key_blocks, value_blocks, decay_blocks))
    retained = retained.reshape(SEQ, HEADS, VALUE_DIM)
    centered = retained - lax.optimization_barrier(jnp.mean(retained, axis=-1, keepdims=True))
    spread = lax.optimization_barrier(jnp.mean(centered * centered, axis=-1, keepdims=True))
    normed = (centered * lax.rsqrt(spread + 1e-06) * norm_gain.reshape(HEADS, VALUE_DIM)).astype(jnp.bfloat16)
    normed = normed.reshape(SEQ, HEADS * VALUE_DIM)
    gated = normed.astype(jnp.float32) * jax.nn.silu(gate_rows.astype(jnp.float32))
    return gated.astype(jnp.bfloat16)
```

```python
import functools

import jax
import jax.numpy as jnp
from jax import lax
from jax.experimental import pallas as pl
from jax.experimental.pallas import tpu as pltpu
from jax.sharding import PartitionSpec as P

KEY_DIM = 256
VALUE_DIM = 512
ROWS = 64
MESH = pl.DeviceIdType.MESH


def wide(row, copies):
    return jnp.concatenate([row] * copies, axis=1)


def kernel(
    peers, blocks, heads,
    q_ref, k_ref, v_ref, g_ref, dec_ref, gain_ref, out_ref,
    tots, gains, wcol, wrow, local,
    pair, lone, chip, arrived, before, after, onward, carry, given,
    tot_send, tot_recv, gain_send, gain_recv, pair_send, pair_recv, chip_send, chip_recv,
    after_send, after_recv, carry_send, carry_recv, given_send, given_recv,
):
    chips = peers // 2
    owned = heads // peers
    half = heads // 2
    tokens = q_ref.shape[0]
    scale = KEY_DIM ** (-0.5)
    me = lax.axis_index("head")
    block = lax.axis_index("ctx")
    x, c = lax.div(me, 2), lax.rem(me, 2)
    sibling = x * 2 + (1 - c)

    barrier = pltpu.get_barrier_semaphore()
    for step in range(1, peers):
        pl.semaphore_signal(
            barrier, inc=1, device_id={"head": lax.rem(me + step, peers)}, device_id_type=MESH
        )

    @pl.when(block > 0)
    def _():
        pl.semaphore_signal(barrier, inc=1, device_id={"ctx": block - 1}, device_id_type=MESH)

    @pl.when(block < blocks - 1)
    def _():
        pl.semaphore_signal(barrier, inc=1, device_id={"ctx": block + 1}, device_id_type=MESH)

    neighbours = jnp.minimum(block, 1) + jnp.minimum(blocks - 1 - block, 1)
    pl.semaphore_wait(barrier, peers - 1 + neighbours)

    def copy_to(src, dst, send, recv, where):
        return pltpu.make_async_remote_copy(
            src_ref=src, dst_ref=dst, send_sem=send, recv_sem=recv,
            device_id=where, device_id_type=MESH,
        )

    dec = dec_ref[...]
    first = lax.broadcasted_iota(jnp.int32, (tokens, tokens), 0)
    second = lax.broadcasted_iota(jnp.int32, (tokens, tokens), 1)
    causal = first >= second
    lower = jnp.where(causal, 1.0, 0.0).astype(jnp.bfloat16)
    upper = jnp.where(first <= second, 1.0, 0.0).astype(jnp.bfloat16)
    ones = jnp.ones((tokens, 128), jnp.bfloat16)
    down = (((0,), (0,)), ((), ()))
    tots[me] = lax.dot_general(dec, ones, down, preferred_element_type=jnp.float32)
    gains[me] = gain_ref[...]

    def tot_copy(step, source):
        return copy_to(
            tots.at[source], tots.at[source], tot_send.at[step], tot_recv.at[source],
            {"head": lax.rem(me + step, peers)},
        )

    def gain_copy(step, source):
        return copy_to(
            gains.at[source], gains.at[source], gain_send.at[step], gain_recv.at[source],
            {"head": lax.rem(me + step, peers)},
        )

    for step in range(1, peers):
        tot_copy(step, me).start()
    for step in range(1, peers):
        gain_copy(step, me).start()

    within = jnp.dot(lower, dec, preferred_element_type=jnp.float32)
    wrow[...] = lax.dot_general(dec, upper, down, preferred_element_type=jnp.float32)
    for h in range(heads):
        wcol[h] = jnp.broadcast_to(within[:, h : h + 1], (tokens, 128))

    def columns(ref, h, size):
        return ref[:, pl.ds(pl.multiple_of(h * size, size), size)]

    def total(device, h, copies):
        return wide(tots[device, pl.ds(h, 1), :], copies)

    def chunk_state(h):
        fade = jnp.exp(tots[me, pl.ds(h, 1), :] - wcol[h])
        keys = columns(k_ref, h, KEY_DIM).astype(jnp.float32) * wide(fade, KEY_DIM // 128)
        return lax.dot_general(
            keys.astype(jnp.bfloat16), columns(v_ref, h, VALUE_DIM), down,
            preferred_element_type=jnp.float32,
        ).astype(jnp.bfloat16)

    def by_rows(body):
        def turn(n, nothing):
            body(pl.ds(pl.multiple_of(n * ROWS, ROWS), ROWS))
            return nothing

        lax.fori_loop(0, KEY_DIM // ROWS, turn, 0)

    def pair_copy(j):
        return copy_to(
            lone.at[j], pair.at[c, j], pair_send.at[j], pair_recv.at[j], {"head": sibling}
        )

    def chip_copy(there, i):
        return copy_to(
            chip.at[there * owned + i], arrived.at[x, i],
            chip_send.at[there * owned + i], chip_recv.at[x, i], {"head": there * 2 + c},
        )

    def far_first(t):
        return lax.rem(x + 1 + lax.div(t, owned), chips), lax.rem(t, owned)

    def join_pair(t):
        there, i = far_first(t)
        j = there * owned + i
        h = (there * 2 + c) * owned + i
        copy_to(
            lone.at[j], pair.at[1 - c, j], pair_send.at[j], pair_recv.at[j], {"head": sibling}
        ).wait_recv()
        fade = jnp.exp(total(x * 2 + 1, h, VALUE_DIM // 128))

        def joined(rows):
            return (
                fade * pair[0, j, rows, :].astype(jnp.float32)
                + pair[1, j, rows, :].astype(jnp.float32)
            ).astype(jnp.bfloat16)

        @pl.when(there == x)
        def _():
            def put(rows):
                arrived[x, i, rows, :] = joined(rows)

            by_rows(put)

        @pl.when(there != x)
        def _():
            def put(rows):
                chip[j, rows, :] = joined(rows)

            by_rows(put)
            chip_copy(there, i).start()

    def states(t, nothing):
        there, i = far_first(t)
        j = there * owned + i
        lone[j] = chunk_state((there * 2 + (1 - c)) * owned + i)
        pair_copy(j).start()
        pair[c, j] = chunk_state((there * 2 + c) * owned + i)

        @pl.when(t == 0)
        def _():
            for step in range(1, peers):
                tot_copy(step, lax.rem(me + step, peers)).wait_recv()

        @pl.when(t > 0)
        def _():
            join_pair(t - 1)

        return nothing

    lax.fori_loop(0, half, states, 0)
    join_pair(half - 1)

    def inside(h):
        gaps = wcol[h] - wrow[pl.ds(h, 1), :]
        damping = jnp.where(causal, jnp.exp(jnp.where(causal, gaps, 0.0)), 0.0)
        scores = lax.dot_general(
            columns(q_ref, h, KEY_DIM), columns(k_ref, h, KEY_DIM), (((1,), (1,)), ((), ())),
            preferred_element_type=jnp.float32,
        )
        weights = (scores * scale * damping).astype(jnp.bfloat16)
        local[:, pl.ds(pl.multiple_of(h * VALUE_DIM, VALUE_DIM), VALUE_DIM)] = jnp.dot(
            weights, columns(v_ref, h, VALUE_DIM), preferred_element_type=jnp.float32
        )

    def after_copy(i):
        return copy_to(
            after.at[i], before.at[i], after_send.at[i], after_recv.at[i], {"ctx": block + 1}
        )

    def carry_copy(there, i):
        return copy_to(
            onward.at[there, i], carry.at[0, x * owned + i],
            carry_send.at[there, i], carry_recv.at[x * owned + i], {"head": there * 2 + c},
        )

    def own_heads(i, nothing):
        h = me * owned + i
        for step in range(1, chips):
            there = lax.rem(x + step, chips)
            copy_to(
                chip.at[there * owned + i], arrived.at[there, i],
                chip_send.at[there * owned + i], chip_recv.at[there, i], {"head": there * 2 + c},
            ).wait_recv()

        @pl.when(block > 0)
        def _():
            copy_to(
                after.at[i], before.at[i], after_send.at[i], after_recv.at[i], {"ctx": block - 1}
            ).wait_recv()

        @pl.when(block == 0)
        def _():
            before[i] = jnp.zeros((KEY_DIM, VALUE_DIM), jnp.bfloat16)

        fades = [
            jnp.exp(total(2 * n, h, VALUE_DIM // 128) + total(2 * n + 1, h, VALUE_DIM // 128))
            for n in range(chips)
        ]

        def put(rows):
            state = before[i, rows, :].astype(jnp.float32)
            for n in range(chips):
                onward[n, i, rows, :] = state.astype(jnp.bfloat16)
                state = fades[n] * state + arrived[n, i, rows, :].astype(jnp.float32)
            after[i, rows, :] = state.astype(jnp.bfloat16)

        by_rows(put)

        @pl.when(block < blocks - 1)
        def _():
            after_copy(i).start()

        for step in range(1, chips):
            carry_copy(lax.rem(x + step, chips), i).start()
        carry[0, x * owned + i] = onward[x, i]

        def local_head(n, nothing):
            inside(i * peers + n)
            return nothing

        lax.fori_loop(0, peers, local_head, 0)
        return nothing

    lax.fori_loop(0, owned, own_heads, 0)

    for step in range(1, peers):
        gain_copy(step, lax.rem(me + step, peers)).wait_recv()

    def finish(device, i, state):
        h = device * owned + i
        inter = jnp.dot(columns(q_ref, h, KEY_DIM), state, preferred_element_type=jnp.float32)
        rise = jnp.exp(wcol[h]) * scale
        retained = columns(local, h, VALUE_DIM) + inter * wide(rise, VALUE_DIM // 128)
        centered = retained - jnp.mean(retained, axis=-1, keepdims=True)
        spread = jnp.mean(centered * centered, axis=-1, keepdims=True)
        gain = gains[device, :, pl.ds(pl.multiple_of(i * VALUE_DIM, VALUE_DIM), VALUE_DIM)]
        normed = (centered * lax.rsqrt(spread + 1e-06) * gain).astype(jnp.bfloat16)
        gate = columns(g_ref, h, VALUE_DIM).astype(jnp.float32)
        out_ref[:, pl.ds(pl.multiple_of(h * VALUE_DIM, VALUE_DIM), VALUE_DIM)] = (
            normed.astype(jnp.float32) * (gate / (1.0 + jnp.exp(-gate)))
        ).astype(jnp.bfloat16)

    def near_first(t):
        return lax.rem(x + lax.rem(t, chips), chips), lax.div(t, chips)

    def given_copy(j):
        return copy_to(
            carry.at[1 - c, j], given.at[j], given_send.at[j], given_recv.at[j],
            {"head": sibling},
        )

    def take_given(t):
        there, i = near_first(t)
        j = there * owned + i
        given_copy(j).wait_recv()
        finish(there * 2 + (1 - c), i, given[j])

    def spread_carry(t, nothing):
        there, i = near_first(t)
        j = there * owned + i
        h = (there * 2 + c) * owned + i

        @pl.when(there != x)
        def _():
            copy_to(
                onward.at[there, i], carry.at[0, j], carry_send.at[there, i], carry_recv.at[j],
                {"head": there * 2 + c},
            ).wait_recv()

        fade = jnp.exp(total(x * 2, h, VALUE_DIM // 128))

        def put(rows):
            carry[1, j, rows, :] = (
                fade * carry[0, j, rows, :].astype(jnp.float32)
                + pair[0, j, rows, :].astype(jnp.float32)
            ).astype(jnp.bfloat16)

        by_rows(put)
        given_copy(j).start()
        finish(there * 2 + c, i, carry[c, j])

        @pl.when(t > 0)
        def _():
            take_given(t - 1)

        return nothing

    lax.fori_loop(0, half, spread_carry, 0)
    take_given(half - 1)

    for step in range(1, peers):
        tot_copy(step, me).wait_send()
        gain_copy(step, me).wait_send()

    def sent(j, nothing):
        pair_copy(j).wait_send()
        given_copy(j).wait_send()
        return nothing

    lax.fori_loop(0, half, sent, 0)

    def sent_far(i, nothing):
        for step in range(1, chips):
            there = lax.rem(x + step, chips)
            chip_copy(there, i).wait_send()
            carry_copy(there, i).wait_send()

        @pl.when(block < blocks - 1)
        def _():
            after_copy(i).wait_send()

        return nothing

    lax.fori_loop(0, owned, sent_far, 0)


def body(peers, blocks, query_rows, key_rows, value_rows, gate_rows, decay_log, norm_gain):
    tokens, heads = decay_log.shape
    chips, owned, half = peers // 2, heads // peers, heads // 2
    state = (KEY_DIM, VALUE_DIM)
    dma = pltpu.SemaphoreType.DMA
    width = norm_gain.shape[0]
    return pl.pallas_call(
        functools.partial(kernel, peers, blocks, heads),
        out_shape=jax.ShapeDtypeStruct(value_rows.shape, jnp.bfloat16),
        in_specs=[pl.BlockSpec(memory_space=pltpu.VMEM)] * 6,
        out_specs=pl.BlockSpec(memory_space=pltpu.VMEM),
        scratch_shapes=[
            pltpu.VMEM((peers, heads, 128), jnp.float32),
            pltpu.VMEM((peers, 1, width), jnp.float32),
            pltpu.VMEM((heads, tokens, 128), jnp.float32),
            pltpu.VMEM((heads, tokens), jnp.float32),
            pltpu.VMEM((tokens, heads * VALUE_DIM), jnp.float32),
            pltpu.VMEM((2, half) + state, jnp.bfloat16),
            pltpu.VMEM((half,) + state, jnp.bfloat16),
            pltpu.VMEM((half,) + state, jnp.bfloat16),
            pltpu.VMEM((chips, owned) + state, jnp.bfloat16),
            pltpu.VMEM((owned,) + state, jnp.bfloat16),
            pltpu.VMEM((owned,) + state, jnp.bfloat16),
            pltpu.VMEM((chips, owned) + state, jnp.bfloat16),
            pltpu.VMEM((2, half) + state, jnp.bfloat16),
            pltpu.VMEM((half,) + state, jnp.bfloat16),
            dma((peers,)), dma((peers,)), dma((peers,)), dma((peers,)),
            dma((half,)), dma((half,)), dma((half,)), dma((chips, owned)),
            dma((owned,)), dma((owned,)), dma((chips, owned)), dma((half,)),
            dma((half,)), dma((half,)),
        ],
        compiler_params=pltpu.CompilerParams(
            collective_id=0, has_side_effects=True, vmem_limit_bytes=52 * 1024 * 1024
        ),
    )(query_rows, key_rows, value_rows, gate_rows, decay_log, norm_gain.reshape(1, width))


def solution(mesh):
    rows = P(("groups", "ctx", "head"), None)
    return jax.shard_map(
        functools.partial(body, mesh.shape["head"], mesh.shape["ctx"]),
        mesh=mesh,
        in_specs=(rows, rows, rows, rows, rows, P("head")),
        out_specs=rows,
        check_vma=False,
    )
```

```python
import functools

import jax
import jax.numpy as jnp
from jax import lax
from jax.experimental import pallas as pl
from jax.experimental.pallas import tpu as pltpu
from jax.sharding import PartitionSpec as P

KEY_DIM = 256
VALUE_DIM = 512
ROWS = 64
PIECES = 2
MESH = pl.DeviceIdType.MESH


def wide(row, copies):
    return jnp.concatenate([row] * copies, axis=1)


def kernel(
    peers, blocks, heads,
    q_hbm, k_hbm, v_hbm, g_hbm, dec_ref, gain_ref, out_ref,
    q_ref, k_ref, v_ref, g_ref, load_sem, tots, gains, wcol, wrow, local,
    pair, lone, chip, arrived, before, after, onward, carry, given,
    tot_send, tot_recv, gain_send, gain_recv, pair_send, pair_recv, chip_send, chip_recv,
    after_send, after_recv, carry_send, carry_recv, given_send, given_recv,
):
    chips = peers // 2
    owned = heads // peers
    half = heads // 2
    tokens = q_ref.shape[0]
    scale = KEY_DIM ** (-0.5)
    me = lax.axis_index("head")
    block = lax.axis_index("ctx")
    x, c = lax.div(me, 2), lax.rem(me, 2)
    sibling = x * 2 + (1 - c)
    last = blocks - 1

    loads = [
        pltpu.make_async_copy(source, target, load_sem.at[n])
        for n, (source, target) in enumerate(
            ((k_hbm, k_ref), (v_hbm, v_ref), (q_hbm, q_ref), (g_hbm, g_ref))
        )
    ]
    for load in loads:
        load.start()

    barrier = pltpu.get_barrier_semaphore()
    for step in range(1, peers):
        pl.semaphore_signal(
            barrier, inc=1, device_id={"head": lax.rem(me + step, peers)}, device_id_type=MESH
        )

    @pl.when(block > 0)
    def _():
        pl.semaphore_signal(barrier, inc=1, device_id={"ctx": block - 1}, device_id_type=MESH)

    @pl.when(block < last)
    def _():
        pl.semaphore_signal(barrier, inc=1, device_id={"ctx": block + 1}, device_id_type=MESH)

    def copy_to(src, dst, send, recv, where):
        return pltpu.make_async_remote_copy(
            src_ref=src, dst_ref=dst, send_sem=send, recv_sem=recv,
            device_id=where, device_id_type=MESH,
        )

    dec = dec_ref[...]
    first = lax.broadcasted_iota(jnp.int32, (tokens, tokens), 0)
    second = lax.broadcasted_iota(jnp.int32, (tokens, tokens), 1)
    causal = first >= second
    lower = jnp.where(causal, 1.0, 0.0).astype(jnp.bfloat16)
    upper = jnp.where(first <= second, 1.0, 0.0).astype(jnp.bfloat16)
    ones = jnp.ones((tokens, 128), jnp.bfloat16)
    down = (((0,), (0,)), ((), ()))
    tots[me] = lax.dot_general(dec, ones, down, preferred_element_type=jnp.float32)
    gains[me] = gain_ref[...]

    def tot_copy(step, source):
        return copy_to(
            tots.at[source], tots.at[source], tot_send.at[step], tot_recv.at[source],
            {"head": lax.rem(me + step, peers)},
        )

    def gain_copy(step, source):
        return copy_to(
            gains.at[source], gains.at[source], gain_send.at[step], gain_recv.at[source],
            {"head": lax.rem(me + step, peers)},
        )

    within = jnp.dot(lower, dec, preferred_element_type=jnp.float32)
    wrow[...] = lax.dot_general(dec, upper, down, preferred_element_type=jnp.float32)
    for h in range(heads):
        wcol[h] = jnp.broadcast_to(within[:, h : h + 1], (tokens, 128))

    neighbours = jnp.minimum(block, 1) + jnp.minimum(blocks - 1 - block, 1)
    pl.semaphore_wait(barrier, peers - 1 + neighbours)

    for step in range(1, peers):
        tot_copy(step, me).start()
    for step in range(1, peers):
        gain_copy(step, me).start()

    def columns(ref, h, size):
        return ref[:, pl.ds(pl.multiple_of(h * size, size), size)]

    def total(device, h, copies):
        return wide(tots[device, pl.ds(h, 1), :], copies)

    def chunk_state(h):
        fade = jnp.exp(tots[me, pl.ds(h, 1), :] - wcol[h])
        keys = columns(k_ref, h, KEY_DIM).astype(jnp.float32) * wide(fade, KEY_DIM // 128)
        return lax.dot_general(
            keys.astype(jnp.bfloat16), columns(v_ref, h, VALUE_DIM), down,
            preferred_element_type=jnp.float32,
        ).astype(jnp.bfloat16)

    def by_rows(body):
        def turn(n, nothing):
            body(pl.ds(pl.multiple_of(n * ROWS, ROWS), ROWS))
            return nothing

        lax.fori_loop(0, KEY_DIM // ROWS, turn, 0)

    def piece(p):
        return pl.ds(p * (KEY_DIM // PIECES), KEY_DIM // PIECES)

    def by_piece_rows(p, body):
        size = KEY_DIM // PIECES

        def turn(n, nothing):
            body(pl.ds(pl.multiple_of(p * size + n * ROWS, ROWS), ROWS))
            return nothing

        lax.fori_loop(0, size // ROWS, turn, 0)

    def pair_copy(j):
        return copy_to(
            lone.at[j], pair.at[c, j], pair_send.at[j], pair_recv.at[j], {"head": sibling}
        )

    def chip_copy(there, i, p):
        j = there * owned + i
        return copy_to(
            chip.at[j, piece(p)], arrived.at[x, i, piece(p)],
            chip_send.at[j, p], chip_recv.at[x, i, p], {"head": there * 2 + c},
        )

    def join_pair(there, i, far):
        j = there * owned + i
        h = (there * 2 + c) * owned + i
        copy_to(
            lone.at[j], pair.at[1 - c, j], pair_send.at[j], pair_recv.at[j], {"head": sibling}
        ).wait_recv()
        fade = jnp.exp(total(x * 2 + 1, h, VALUE_DIM // 128))
        for p in range(PIECES):

            def put(rows):
                joined = (
                    fade * pair[0, j, rows, :].astype(jnp.float32)
                    + pair[1, j, rows, :].astype(jnp.float32)
                ).astype(jnp.bfloat16)
                if far:
                    chip[j, rows, :] = joined
                else:
                    arrived[x, i, rows, :] = joined

            by_piece_rows(p, put)
            if far:
                chip_copy(there, i, p).start()

    def states(there, i):
        j = there * owned + i
        lone[j] = chunk_state((there * 2 + (1 - c)) * owned + i)
        pair_copy(j).start()
        pair[c, j] = chunk_state((there * 2 + c) * owned + i)

    def far_place(t):
        return lax.rem(x + 1 + lax.rem(t, chips - 1), chips), lax.div(t, chips - 1)

    def far_states(t, nothing):
        there, i = far_place(t)
        states(there, i)

        @pl.when(t == 0)
        def _():
            for step in range(1, peers):
                tot_copy(step, lax.rem(me + step, peers)).wait_recv()

        @pl.when(t > 0)
        def _():
            before_there, before_i = far_place(t - 1)
            join_pair(before_there, before_i, True)

        return nothing

    loads[0].wait()
    loads[1].wait()
    far = (chips - 1) * owned
    lax.fori_loop(0, far, far_states, 0)
    states(x, 0)
    last_there, last_i = far_place(far - 1)
    join_pair(last_there, last_i, True)
    loads[2].wait()
    loads[3].wait()

    def inside(h):
        gaps = wcol[h] - wrow[pl.ds(h, 1), :]
        damping = jnp.where(causal, jnp.exp(jnp.where(causal, gaps, 0.0)), 0.0)
        scores = lax.dot_general(
            columns(q_ref, h, KEY_DIM), columns(k_ref, h, KEY_DIM), (((1,), (1,)), ((), ())),
            preferred_element_type=jnp.float32,
        )
        weights = (scores * scale * damping).astype(jnp.bfloat16)
        local[:, pl.ds(pl.multiple_of(h * VALUE_DIM, VALUE_DIM), VALUE_DIM)] = jnp.dot(
            weights, columns(v_ref, h, VALUE_DIM), preferred_element_type=jnp.float32
        )

    def after_copy(i, p):
        return copy_to(
            after.at[i, piece(p)], before.at[i, piece(p)],
            after_send.at[i, p], after_recv.at[i, p], {"ctx": block + 1},
        )

    def carry_copy(there, i, p):
        j = x * owned + i
        return copy_to(
            onward.at[there, i, piece(p)], carry.at[0, j, piece(p)],
            carry_send.at[there, i, p], carry_recv.at[j, p], {"head": there * 2 + c},
        )

    def chain(i, p):
        h = me * owned + i
        for step in range(1, chips):
            there = lax.rem(x + step, chips)
            copy_to(
                chip.at[there * owned + i, piece(p)], arrived.at[there, i, piece(p)],
                chip_send.at[there * owned + i, p], chip_recv.at[there, i, p],
                {"head": there * 2 + c},
            ).wait_recv()

        @pl.when(block > 0)
        def _():
            copy_to(
                after.at[i, piece(p)], before.at[i, piece(p)],
                after_send.at[i, p], after_recv.at[i, p], {"ctx": block - 1},
            ).wait_recv()

        @pl.when(block == 0)
        def _():
            before[i, piece(p)] = jnp.zeros((KEY_DIM // PIECES, VALUE_DIM), jnp.bfloat16)

        fades = [
            jnp.exp(total(2 * n, h, VALUE_DIM // 128) + total(2 * n + 1, h, VALUE_DIM // 128))
            for n in range(chips)
        ]

        def put(rows):
            state = before[i, rows, :].astype(jnp.float32)
            for n in range(chips):
                onward[n, i, rows, :] = state.astype(jnp.bfloat16)
                state = fades[n] * state + arrived[n, i, rows, :].astype(jnp.float32)
            after[i, rows, :] = state.astype(jnp.bfloat16)

        by_piece_rows(p, put)

        @pl.when(block < last)
        def _():
            after_copy(i, p).start()

        @pl.when(block == last)
        def _():
            send_carry(i, p)

    def send_carry(i, p):
        for step in range(1, chips):
            carry_copy(lax.rem(x + step, chips), i, p).start()

    def send_carries(i, nothing):
        for p in range(PIECES):
            send_carry(i, p)
        return nothing

    def locals_of(i):
        def local_head(n, nothing):
            inside(n * owned + i)
            return nothing

        lax.fori_loop(0, peers, local_head, 0)

    delay = jnp.maximum(owned - 1 - block, 0)

    def own_heads(i, nothing):
        @pl.when(block > 0)
        def _():
            locals_of(i)

        join_pair(x, i, False)
        for p in range(PIECES):
            chain(i, p)
        carry[0, x * owned + i] = onward[x, i]

        @pl.when(jnp.logical_and(block < last, i >= delay))
        def _():
            send_carries(i - delay, 0)

        @pl.when(i < owned - 1)
        def _():
            states(x, i + 1)

        @pl.when(block == 0)
        def _():
            locals_of(i)

        @pl.when(jnp.logical_and(block == last, i > 0))
        def _():
            spread_all(i - 1, 0)

        return nothing

    def finish(device, i, state):
        h = device * owned + i
        inter = jnp.dot(columns(q_ref, h, KEY_DIM), state, preferred_element_type=jnp.float32)
        rise = jnp.exp(wcol[h]) * scale
        retained = columns(local, h, VALUE_DIM) + inter * wide(rise, VALUE_DIM // 128)
        centered = retained - jnp.mean(retained, axis=-1, keepdims=True)
        spread = jnp.mean(centered * centered, axis=-1, keepdims=True)
        gain = gains[device, :, pl.ds(pl.multiple_of(i * VALUE_DIM, VALUE_DIM), VALUE_DIM)]
        normed = (centered * lax.rsqrt(spread + 1e-06) * gain).astype(jnp.bfloat16)
        gate = columns(g_ref, h, VALUE_DIM).astype(jnp.float32)
        out_ref[:, pl.ds(pl.multiple_of(h * VALUE_DIM, VALUE_DIM), VALUE_DIM)] = (
            normed.astype(jnp.float32) * (gate / (1.0 + jnp.exp(-gate)))
        ).astype(jnp.bfloat16)

    def given_copy(j):
        return copy_to(
            carry.at[1 - c, j], given.at[j], given_send.at[j], given_recv.at[j],
            {"head": sibling},
        )

    def take_given(there, i):
        j = there * owned + i
        given_copy(j).wait_recv()
        finish(there * 2 + (1 - c), i, given[j])

    def spread(there, i, far):
        j = there * owned + i
        h = (there * 2 + c) * owned + i
        fade = jnp.exp(total(x * 2, h, VALUE_DIM // 128))
        for p in range(PIECES):
            if far:
                copy_to(
                    onward.at[there, i, piece(p)], carry.at[0, j, piece(p)],
                    carry_send.at[there, i, p], carry_recv.at[j, p], {"head": there * 2 + c},
                ).wait_recv()

            def put(rows):
                carry[1, j, rows, :] = (
                    fade * carry[0, j, rows, :].astype(jnp.float32)
                    + pair[0, j, rows, :].astype(jnp.float32)
                ).astype(jnp.bfloat16)

            by_piece_rows(p, put)
        given_copy(j).start()
        finish(there * 2 + c, i, carry[c, j])

    def spread_all(i, nothing):
        spread(x, i, False)
        take_given(x, i)

        def turn(step, nothing):
            there = lax.rem(x + step, chips)
            spread(there, i, True)
            take_given(there, i)
            return nothing

        lax.fori_loop(1, chips, turn, 0)
        return nothing

    for step in range(1, peers):
        gain_copy(step, lax.rem(me + step, peers)).wait_recv()

    lax.fori_loop(0, owned, own_heads, 0)

    @pl.when(block < last)
    def _():
        lax.fori_loop(jnp.maximum(owned - delay, 0), owned, send_carries, 0)

    lax.fori_loop(jnp.where(block == last, owned - 1, 0), owned, spread_all, 0)

    for step in range(1, peers):
        tot_copy(step, me).wait_send()
        gain_copy(step, me).wait_send()

    def sent(j, nothing):
        pair_copy(j).wait_send()
        given_copy(j).wait_send()
        return nothing

    lax.fori_loop(0, half, sent, 0)

    def sent_far(i, nothing):
        for step in range(1, chips):
            there = lax.rem(x + step, chips)
            for p in range(PIECES):
                chip_copy(there, i, p).wait_send()
                carry_copy(there, i, p).wait_send()

        @pl.when(block < last)
        def _():
            for p in range(PIECES):
                after_copy(i, p).wait_send()

        return nothing

    lax.fori_loop(0, owned, sent_far, 0)


def body(peers, blocks, query_rows, key_rows, value_rows, gate_rows, decay_log, norm_gain):
    tokens, heads = decay_log.shape
    chips, owned, half = peers // 2, heads // peers, heads // 2
    state = (KEY_DIM, VALUE_DIM)
    dma = pltpu.SemaphoreType.DMA
    width = norm_gain.shape[0]
    return pl.pallas_call(
        functools.partial(kernel, peers, blocks, heads),
        out_shape=jax.ShapeDtypeStruct(value_rows.shape, jnp.bfloat16),
        in_specs=[pl.BlockSpec(memory_space=pl.ANY)] * 4
        + [pl.BlockSpec(memory_space=pltpu.VMEM)] * 2,
        out_specs=pl.BlockSpec(memory_space=pltpu.VMEM),
        scratch_shapes=[
            pltpu.VMEM(query_rows.shape, jnp.bfloat16),
            pltpu.VMEM(key_rows.shape, jnp.bfloat16),
            pltpu.VMEM(value_rows.shape, jnp.bfloat16),
            pltpu.VMEM(gate_rows.shape, jnp.bfloat16),
            dma((4,)),
            pltpu.VMEM((peers, heads, 128), jnp.float32),
            pltpu.VMEM((peers, 1, width), jnp.float32),
            pltpu.VMEM((heads, tokens, 128), jnp.float32),
            pltpu.VMEM((heads, tokens), jnp.float32),
            pltpu.VMEM((tokens, heads * VALUE_DIM), jnp.float32),
            pltpu.VMEM((2, half) + state, jnp.bfloat16),
            pltpu.VMEM((half,) + state, jnp.bfloat16),
            pltpu.VMEM((half,) + state, jnp.bfloat16),
            pltpu.VMEM((chips, owned) + state, jnp.bfloat16),
            pltpu.VMEM((owned,) + state, jnp.bfloat16),
            pltpu.VMEM((owned,) + state, jnp.bfloat16),
            pltpu.VMEM((chips, owned) + state, jnp.bfloat16),
            pltpu.VMEM((2, half) + state, jnp.bfloat16),
            pltpu.VMEM((half,) + state, jnp.bfloat16),
            dma((peers,)), dma((peers,)), dma((peers,)), dma((peers,)),
            dma((half,)), dma((half,)),
            dma((half, PIECES)), dma((chips, owned, PIECES)),
            dma((owned, PIECES)), dma((owned, PIECES)),
            dma((chips, owned, PIECES)), dma((half, PIECES)),
            dma((half,)), dma((half,)),
        ],
        compiler_params=pltpu.CompilerParams(
            collective_id=0, has_side_effects=True, vmem_limit_bytes=60 * 1024 * 1024
        ),
    )(query_rows, key_rows, value_rows, gate_rows, decay_log, norm_gain.reshape(1, width))


def solution(mesh):
    rows = P(("groups", "ctx", "head"), None)
    return jax.shard_map(
        functools.partial(body, mesh.shape["head"], mesh.shape["ctx"]),
        mesh=mesh,
        in_specs=(rows, rows, rows, rows, rows, P("head")),
        out_specs=rows,
        check_vma=False,
    )
```

```python
import functools

import jax
import jax.numpy as jnp
from jax import lax
from jax.experimental import pallas as pl
from jax.experimental.pallas import tpu as pltpu
from jax.sharding import PartitionSpec as P

KEY_DIM = 256
VALUE_DIM = 512
ROWS = 64
PIECES = 2
PARTS = 8
MESH = pl.DeviceIdType.MESH


def wide(row, copies):
    return jnp.concatenate([row] * copies, axis=1)


def kernel(
    peers, blocks, heads,
    q_hbm, k_hbm, v_hbm, g_hbm, dec_hbm, gain_hbm, out_hbm,
    q_ref, k_ref, v_ref, g_ref, dec_ref, out_ref, load_sem, out_sem, tots, gains, wcol, wrow, local,
    pair, lone, chip, arrived, before, after, onward, carry, given,
    tot_send, tot_recv, gain_send, gain_recv, pair_send, pair_recv, chip_send, chip_recv,
    after_send, after_recv, carry_send, carry_recv, given_send, given_recv,
):
    chips = peers // 2
    owned = heads // peers
    half = heads // 2
    tokens = q_ref.shape[0]
    scale = KEY_DIM ** (-0.5)
    me = lax.axis_index("head")
    block = lax.axis_index("ctx")
    x, c = lax.div(me, 2), lax.rem(me, 2)
    sibling = x * 2 + (1 - c)
    last = blocks - 1

    loads = [
        pltpu.make_async_copy(source, target, load_sem.at[n])
        for n, (source, target) in enumerate(
            (
                (dec_hbm, dec_ref), (k_hbm, k_ref), (v_hbm, v_ref),
                (gain_hbm, gains.at[me]), (q_hbm, q_ref), (g_hbm, g_ref),
            )
        )
    ]
    for load in loads:
        load.start()

    barrier = pltpu.get_barrier_semaphore()
    for step in range(1, peers):
        pl.semaphore_signal(
            barrier, inc=1, device_id={"head": lax.rem(me + step, peers)}, device_id_type=MESH
        )

    @pl.when(block > 0)
    def _():
        pl.semaphore_signal(barrier, inc=1, device_id={"ctx": block - 1}, device_id_type=MESH)

    @pl.when(block < last)
    def _():
        pl.semaphore_signal(barrier, inc=1, device_id={"ctx": block + 1}, device_id_type=MESH)

    def copy_to(src, dst, send, recv, where):
        return pltpu.make_async_remote_copy(
            src_ref=src, dst_ref=dst, send_sem=send, recv_sem=recv,
            device_id=where, device_id_type=MESH,
        )

    loads[0].wait()
    dec = dec_ref[...]
    first = lax.broadcasted_iota(jnp.int32, (tokens, tokens), 0)
    second = lax.broadcasted_iota(jnp.int32, (tokens, tokens), 1)
    causal = first >= second
    lower = jnp.where(causal, 1.0, 0.0).astype(jnp.bfloat16)
    upper = jnp.where(first <= second, 1.0, 0.0).astype(jnp.bfloat16)
    ones = jnp.ones((tokens, 128), jnp.bfloat16)
    down = (((0,), (0,)), ((), ()))
    tots[me] = jnp.dot(dec, ones, preferred_element_type=jnp.float32)

    def tot_copy(step, source):
        return copy_to(
            tots.at[source], tots.at[source], tot_send.at[step], tot_recv.at[source],
            {"head": lax.rem(me + step, peers)},
        )

    def gain_copy(step, source):
        return copy_to(
            gains.at[source], gains.at[source], gain_send.at[step], gain_recv.at[source],
            {"head": lax.rem(me + step, peers)},
        )

    within = lax.dot_general(
        lower, dec, (((1,), (1,)), ((), ())), preferred_element_type=jnp.float32
    )
    wrow[...] = jnp.dot(dec, upper, preferred_element_type=jnp.float32)
    for h in range(heads):
        wcol[h] = jnp.broadcast_to(within[:, h : h + 1], (tokens, 128))

    def columns(ref, h, size):
        return ref[:, pl.ds(pl.multiple_of(h * size, size), size)]

    def total(device, h, copies):
        return wide(tots[device, pl.ds(h, 1), :], copies)

    def chunk_state(h):
        fade = jnp.exp(tots[me, pl.ds(h, 1), :] - wcol[h])
        keys = columns(k_ref, h, KEY_DIM).astype(jnp.float32) * wide(fade, KEY_DIM // 128)
        return lax.dot_general(
            keys.astype(jnp.bfloat16), columns(v_ref, h, VALUE_DIM), down,
            preferred_element_type=jnp.float32,
        ).astype(jnp.bfloat16)

    def by_rows(body):
        def turn(n, nothing):
            body(pl.ds(pl.multiple_of(n * ROWS, ROWS), ROWS))
            return nothing

        lax.fori_loop(0, KEY_DIM // ROWS, turn, 0)

    def piece(p):
        return pl.ds(p * (KEY_DIM // PIECES), KEY_DIM // PIECES)

    def by_piece_rows(p, body):
        size = KEY_DIM // PIECES

        def turn(n, nothing):
            body(pl.ds(pl.multiple_of(p * size + n * ROWS, ROWS), ROWS))
            return nothing

        lax.fori_loop(0, size // ROWS, turn, 0)

    def pair_copy(j):
        return copy_to(
            lone.at[j], pair.at[c, j], pair_send.at[j], pair_recv.at[j], {"head": sibling}
        )

    def chip_copy(there, i, p):
        j = there * owned + i
        return copy_to(
            chip.at[j, piece(p)], arrived.at[x, i, piece(p)],
            chip_send.at[j, p], chip_recv.at[x, i, p], {"head": there * 2 + c},
        )

    def join_pair(there, i, far):
        j = there * owned + i
        h = (there * 2 + c) * owned + i
        copy_to(
            lone.at[j], pair.at[1 - c, j], pair_send.at[j], pair_recv.at[j], {"head": sibling}
        ).wait_recv()
        fade = jnp.exp(total(x * 2 + 1, h, VALUE_DIM // 128))
        for p in range(PIECES):

            def put(rows):
                joined = (
                    fade * pair[0, j, rows, :].astype(jnp.float32)
                    + pair[1, j, rows, :].astype(jnp.float32)
                ).astype(jnp.bfloat16)
                if far:
                    chip[j, rows, :] = joined
                else:
                    arrived[x, i, rows, :] = joined

            by_piece_rows(p, put)
            if far:
                chip_copy(there, i, p).start()

    def make_states(there, i):
        j = there * owned + i
        lone[j] = chunk_state((there * 2 + (1 - c)) * owned + i)
        pair[c, j] = chunk_state((there * 2 + c) * owned + i)

    def states(there, i):
        j = there * owned + i
        lone[j] = chunk_state((there * 2 + (1 - c)) * owned + i)
        pair_copy(j).start()
        pair[c, j] = chunk_state((there * 2 + c) * owned + i)

    def far_place(t):
        return lax.rem(x + 1 + lax.rem(t, chips - 1), chips), lax.div(t, chips - 1)

    def tot_arrived(source):
        copy_to(
            tots.at[source], tots.at[source], tot_send.at[0], tot_recv.at[source],
            {"head": sibling},
        ).wait_recv()

    loads[1].wait()
    loads[2].wait()
    head_there, head_i = far_place(0)
    make_states(head_there, head_i)
    neighbours = jnp.minimum(block, 1) + jnp.minimum(blocks - 1 - block, 1)
    pl.semaphore_wait(barrier, peers - 1 + neighbours)
    for step in range(1, peers):
        tot_copy(step, me).start()
    pair_copy(head_there * owned + head_i).start()
    tot_arrived(sibling)
    join_pair(head_there, head_i, True)

    def far_states(t, nothing):
        there, i = far_place(t)
        states(there, i)

        @pl.when(t > 1)
        def _():
            before_there, before_i = far_place(t - 1)
            join_pair(before_there, before_i, True)

        return nothing

    far = (chips - 1) * owned
    lax.fori_loop(1, far, far_states, 0)
    states(x, 0)
    if far > 1:
        last_there, last_i = far_place(far - 1)
        join_pair(last_there, last_i, True)
    for load in loads[3:]:
        load.wait()
    for step in range(1, peers):
        gain_copy(step, me).start()
    for source in range(peers):

        @pl.when(x != source // 2)
        def _():
            tot_arrived(source)

    def inside(h):
        gaps = wcol[h] - wrow[pl.ds(h, 1), :]
        damping = jnp.where(causal, jnp.exp(jnp.where(causal, gaps, 0.0)), 0.0)
        scores = lax.dot_general(
            columns(q_ref, h, KEY_DIM), columns(k_ref, h, KEY_DIM), (((1,), (1,)), ((), ())),
            preferred_element_type=jnp.float32,
        )
        weights = (scores * scale * damping).astype(jnp.bfloat16)
        local[:, pl.ds(pl.multiple_of(h * VALUE_DIM, VALUE_DIM), VALUE_DIM)] = jnp.dot(
            weights, columns(v_ref, h, VALUE_DIM), preferred_element_type=jnp.float32
        )

    def after_copy(i, p):
        return copy_to(
            after.at[i, piece(p)], before.at[i, piece(p)],
            after_send.at[i, p], after_recv.at[i, p], {"ctx": block + 1},
        )

    def carry_copy(there, i, p):
        j = x * owned + i
        return copy_to(
            onward.at[there, i, piece(p)], carry.at[0, j, piece(p)],
            carry_send.at[there, i, p], carry_recv.at[j, p], {"head": there * 2 + c},
        )

    def chain(i, p):
        h = me * owned + i
        for step in range(1, chips):
            there = lax.rem(x + step, chips)
            copy_to(
                chip.at[there * owned + i, piece(p)], arrived.at[there, i, piece(p)],
                chip_send.at[there * owned + i, p], chip_recv.at[there, i, p],
                {"head": there * 2 + c},
            ).wait_recv()

        @pl.when(block > 0)
        def _():
            copy_to(
                after.at[i, piece(p)], before.at[i, piece(p)],
                after_send.at[i, p], after_recv.at[i, p], {"ctx": block - 1},
            ).wait_recv()

        @pl.when(block == 0)
        def _():
            before[i, piece(p)] = jnp.zeros((KEY_DIM // PIECES, VALUE_DIM), jnp.bfloat16)

        fades = [
            jnp.exp(total(2 * n, h, VALUE_DIM // 128) + total(2 * n + 1, h, VALUE_DIM // 128))
            for n in range(chips)
        ]

        def put(rows):
            state = before[i, rows, :].astype(jnp.float32)
            for n in range(chips):
                onward[n, i, rows, :] = state.astype(jnp.bfloat16)
                state = fades[n] * state + arrived[n, i, rows, :].astype(jnp.float32)
            after[i, rows, :] = state.astype(jnp.bfloat16)

        by_piece_rows(p, put)

        @pl.when(block < last)
        def _():
            after_copy(i, p).start()

        for step in range(1, chips):
            carry_copy(lax.rem(x + step, chips), i, p).start()

    def locals_of(i):
        def local_head(n, nothing):
            inside(n * owned + i)
            return nothing

        lax.fori_loop(0, peers, local_head, 0)

    def own_heads(i, nothing):
        @pl.when(block > 0)
        def _():
            locals_of(i)

        join_pair(x, i, False)
        for p in range(PIECES):
            chain(i, p)
        carry[0, x * owned + i] = onward[x, i]

        @pl.when(i < owned - 1)
        def _():
            states(x, i + 1)

        @pl.when(block == 0)
        def _():
            locals_of(i)

        @pl.when(jnp.logical_and(block == last, i > 0))
        def _():
            spread_all(i - 1, 0)

        return nothing

    def out_copy(h):
        place = pl.ds(pl.multiple_of(h * VALUE_DIM, VALUE_DIM), VALUE_DIM)
        return pltpu.make_async_copy(
            out_ref.at[:, place], out_hbm.at[:, place], out_sem.at[h]
        )

    def finish(device, i, state):
        h = device * owned + i
        inter = jnp.dot(columns(q_ref, h, KEY_DIM), state, preferred_element_type=jnp.float32)
        rise = jnp.exp(wcol[h]) * scale
        retained = columns(local, h, VALUE_DIM) + inter * wide(rise, VALUE_DIM // 128)
        centered = retained - jnp.mean(retained, axis=-1, keepdims=True)
        spread = jnp.mean(centered * centered, axis=-1, keepdims=True)
        gain = gains[device, :, pl.ds(pl.multiple_of(i * VALUE_DIM, VALUE_DIM), VALUE_DIM)]
        normed = (centered * lax.rsqrt(spread + 1e-06) * gain).astype(jnp.bfloat16)
        gate = columns(g_ref, h, VALUE_DIM).astype(jnp.float32)
        out_ref[:, pl.ds(pl.multiple_of(h * VALUE_DIM, VALUE_DIM), VALUE_DIM)] = (
            normed.astype(jnp.float32) * (gate / (1.0 + jnp.exp(-gate)))
        ).astype(jnp.bfloat16)
        out_copy(h).start()

    def given_copy(j, p):
        return copy_to(
            carry.at[1 - c, j, piece(p)], given.at[j, piece(p)],
            given_send.at[j, p], given_recv.at[j, p], {"head": sibling},
        )

    def take_given(there, i):
        j = there * owned + i
        for p in range(PIECES):
            given_copy(j, p).wait_recv()
        finish(there * 2 + (1 - c), i, given[j])

    def spread(there, i, far):
        j = there * owned + i
        h = (there * 2 + c) * owned + i
        fade = jnp.exp(total(x * 2, h, VALUE_DIM // 128))
        for p in range(PIECES):
            if far:
                copy_to(
                    onward.at[there, i, piece(p)], carry.at[0, j, piece(p)],
                    carry_send.at[there, i, p], carry_recv.at[j, p], {"head": there * 2 + c},
                ).wait_recv()

            def put(rows):
                carry[1, j, rows, :] = (
                    fade * carry[0, j, rows, :].astype(jnp.float32)
                    + pair[0, j, rows, :].astype(jnp.float32)
                ).astype(jnp.bfloat16)

            by_piece_rows(p, put)
            given_copy(j, p).start()
        finish(there * 2 + c, i, carry[c, j])

    def spread_all(i, nothing):
        spread(x, i, False)
        take_given(x, i)

        def turn(step, nothing):
            there = lax.rem(x + step, chips)
            spread(there, i, True)
            take_given(there, i)
            return nothing

        lax.fori_loop(1, chips, turn, 0)
        return nothing

    for step in range(1, peers):
        gain_copy(step, lax.rem(me + step, peers)).wait_recv()

    lax.fori_loop(0, owned, own_heads, 0)

    lax.fori_loop(jnp.where(block == last, owned - 1, 0), owned, spread_all, 0)

    def written(h, nothing):
        out_copy(h).wait()
        return nothing

    for step in range(1, peers):
        tot_copy(step, me).wait_send()
        gain_copy(step, me).wait_send()

    def sent(j, nothing):
        pair_copy(j).wait_send()
        for p in range(PIECES):
            given_copy(j, p).wait_send()
        return nothing

    lax.fori_loop(0, half, sent, 0)

    def sent_far(i, nothing):
        for step in range(1, chips):
            there = lax.rem(x + step, chips)
            for p in range(PIECES):
                chip_copy(there, i, p).wait_send()
                carry_copy(there, i, p).wait_send()

        @pl.when(block < last)
        def _():
            for p in range(PIECES):
                after_copy(i, p).wait_send()

        return nothing

    lax.fori_loop(0, owned, sent_far, 0)
    lax.fori_loop(0, heads, written, 0)


def rewrite(source, target, sem):
    rows = source.shape[0] // PARTS
    copies = [
        pltpu.make_async_copy(
            source.at[pl.ds(n * rows, rows)], target.at[pl.ds(n * rows, rows)], sem.at[n]
        )
        for n in range(PARTS)
    ]
    for copy in copies:
        copy.start()
    for copy in copies:
        copy.wait()


def body(peers, blocks, query_rows, key_rows, value_rows, gate_rows, decay_log, norm_gain):
    tokens, heads = decay_log.shape
    chips, owned, half = peers // 2, heads // peers, heads // 2
    state = (KEY_DIM, VALUE_DIM)
    dma = pltpu.SemaphoreType.DMA
    width = norm_gain.shape[0]
    retained = pl.pallas_call(
        functools.partial(kernel, peers, blocks, heads),
        out_shape=jax.ShapeDtypeStruct(value_rows.shape, jnp.bfloat16),
        in_specs=[pl.BlockSpec(memory_space=pl.ANY)] * 6,
        out_specs=pl.BlockSpec(memory_space=pl.ANY),
        scratch_shapes=[
            pltpu.VMEM(query_rows.shape, jnp.bfloat16),
            pltpu.VMEM(key_rows.shape, jnp.bfloat16),
            pltpu.VMEM(value_rows.shape, jnp.bfloat16),
            pltpu.VMEM(gate_rows.shape, jnp.bfloat16),
            pltpu.VMEM((heads, tokens), jnp.bfloat16),
            pltpu.VMEM(value_rows.shape, jnp.bfloat16),
            dma((6,)), dma((heads,)),
            pltpu.VMEM((peers, heads, 128), jnp.float32),
            pltpu.VMEM((peers, 1, width), jnp.float32),
            pltpu.VMEM((heads, tokens, 128), jnp.float32),
            pltpu.VMEM((heads, tokens), jnp.float32),
            pltpu.VMEM((tokens, heads * VALUE_DIM), jnp.float32),
            pltpu.VMEM((2, half) + state, jnp.bfloat16),
            pltpu.VMEM((half,) + state, jnp.bfloat16),
            pltpu.VMEM((half,) + state, jnp.bfloat16),
            pltpu.VMEM((chips, owned) + state, jnp.bfloat16),
            pltpu.VMEM((owned,) + state, jnp.bfloat16),
            pltpu.VMEM((owned,) + state, jnp.bfloat16),
            pltpu.VMEM((chips, owned) + state, jnp.bfloat16),
            pltpu.VMEM((2, half) + state, jnp.bfloat16),
            pltpu.VMEM((half,) + state, jnp.bfloat16),
            dma((peers,)), dma((peers,)), dma((peers,)), dma((peers,)),
            dma((half,)), dma((half,)),
            dma((half, PIECES)), dma((chips, owned, PIECES)),
            dma((owned, PIECES)), dma((owned, PIECES)),
            dma((chips, owned, PIECES)), dma((half, PIECES)),
            dma((half, PIECES)), dma((half, PIECES)),
        ],
        compiler_params=pltpu.CompilerParams(
            collective_id=0, has_side_effects=True, vmem_limit_bytes=60 * 1024 * 1024
        ),
    )(query_rows, key_rows, value_rows, gate_rows, decay_log.T, norm_gain.reshape(1, width))
    return pl.pallas_call(
        rewrite,
        out_shape=jax.ShapeDtypeStruct(retained.shape, retained.dtype),
        in_specs=[pl.BlockSpec(memory_space=pl.ANY)],
        out_specs=pl.BlockSpec(memory_space=pl.ANY),
        scratch_shapes=[dma((PARTS,))],
    )(retained)


def solution(mesh):
    rows = P(("groups", "ctx", "head"), None)
    return jax.shard_map(
        functools.partial(body, mesh.shape["head"], mesh.shape["ctx"]),
        mesh=mesh,
        in_specs=(rows, rows, rows, rows, rows, P("head")),
        out_specs=rows,
        check_vma=False,
    )
```

```python
import functools

import jax
import jax.numpy as jnp
from jax import lax
from jax.experimental import pallas as pl
from jax.experimental.pallas import tpu as pltpu
from jax.sharding import PartitionSpec as P

KEY_DIM = 256
VALUE_DIM = 512
ROWS = 64
PIECES = 2
PARTS = 8
MESH = pl.DeviceIdType.MESH


def wide(row, copies):
    return jnp.concatenate([row] * copies, axis=1)


def kernel(
    peers, blocks, heads,
    q_hbm, k_hbm, v_hbm, g_hbm, dec_hbm, gain_hbm, out_hbm,
    q_ref, k_ref, v_ref, g_ref, dec_ref, out_ref, load_sem, out_sem, tots, gains, wcol, wrow, local,
    pair, lone, chip, arrived, before, after, onward, carry, given,
    tot_send, tot_recv, gain_send, gain_recv, pair_send, pair_recv, chip_send, chip_recv,
    after_send, after_recv, carry_send, carry_recv, given_send, given_recv,
):
    chips = peers // 2
    owned = heads // peers
    half = heads // 2
    tokens = q_ref.shape[0]
    scale = KEY_DIM ** (-0.5)
    me = lax.axis_index("head")
    block = lax.axis_index("ctx")
    x, c = lax.div(me, 2), lax.rem(me, 2)
    sibling = x * 2 + (1 - c)
    last = blocks - 1

    loads = [
        pltpu.make_async_copy(source, target, load_sem.at[n])
        for n, (source, target) in enumerate(
            (
                (dec_hbm, dec_ref), (k_hbm, k_ref), (v_hbm, v_ref),
                (gain_hbm, gains.at[me]), (q_hbm, q_ref), (g_hbm, g_ref),
            )
        )
    ]
    for load in loads:
        load.start()

    barrier = pltpu.get_barrier_semaphore()
    for step in range(1, peers):
        pl.semaphore_signal(
            barrier, inc=1, device_id={"head": lax.rem(me + step, peers)}, device_id_type=MESH
        )

    @pl.when(block > 0)
    def _():
        pl.semaphore_signal(barrier, inc=1, device_id={"ctx": block - 1}, device_id_type=MESH)

    @pl.when(block < last)
    def _():
        pl.semaphore_signal(barrier, inc=1, device_id={"ctx": block + 1}, device_id_type=MESH)

    def copy_to(src, dst, send, recv, where):
        return pltpu.make_async_remote_copy(
            src_ref=src, dst_ref=dst, send_sem=send, recv_sem=recv,
            device_id=where, device_id_type=MESH,
        )

    loads[0].wait()
    dec = dec_ref[...]
    first = lax.broadcasted_iota(jnp.int32, (tokens, tokens), 0)
    second = lax.broadcasted_iota(jnp.int32, (tokens, tokens), 1)
    causal = first >= second
    lower = jnp.where(causal, 1.0, 0.0).astype(jnp.bfloat16)
    upper = jnp.where(first <= second, 1.0, 0.0).astype(jnp.bfloat16)
    ones = jnp.ones((tokens, 128), jnp.bfloat16)
    down = (((0,), (0,)), ((), ()))
    tots[me] = jnp.dot(dec, ones, preferred_element_type=jnp.float32)

    def tot_copy(step, source):
        return copy_to(
            tots.at[source], tots.at[source], tot_send.at[step], tot_recv.at[source],
            {"head": lax.rem(me + step, peers)},
        )

    def gain_copy(step, source):
        return copy_to(
            gains.at[source], gains.at[source], gain_send.at[step], gain_recv.at[source],
            {"head": lax.rem(me + step, peers)},
        )

    within = lax.dot_general(
        lower, dec, (((1,), (1,)), ((), ())), preferred_element_type=jnp.float32
    )
    wrow[...] = jnp.dot(dec, upper, preferred_element_type=jnp.float32)
    for h in range(heads):
        wcol[h] = jnp.broadcast_to(within[:, h : h + 1], (tokens, 128))

    def columns(ref, h, size):
        return ref[:, pl.ds(pl.multiple_of(h * size, size), size)]

    def total(device, h, copies):
        return wide(tots[device, pl.ds(h, 1), :], copies)

    def chunk_state(h):
        fade = jnp.exp(tots[me, pl.ds(h, 1), :] - wcol[h])
        keys = columns(k_ref, h, KEY_DIM).astype(jnp.float32) * wide(fade, KEY_DIM // 128)
        return lax.dot_general(
            keys.astype(jnp.bfloat16), columns(v_ref, h, VALUE_DIM), down,
            preferred_element_type=jnp.float32,
        ).astype(jnp.bfloat16)

    def by_rows(body):
        def turn(n, nothing):
            body(pl.ds(pl.multiple_of(n * ROWS, ROWS), ROWS))
            return nothing

        lax.fori_loop(0, KEY_DIM // ROWS, turn, 0)

    def piece(p):
        return pl.ds(p * (KEY_DIM // PIECES), KEY_DIM // PIECES)

    def by_piece_rows(p, body):
        size = KEY_DIM // PIECES

        def turn(n, nothing):
            body(pl.ds(pl.multiple_of(p * size + n * ROWS, ROWS), ROWS))
            return nothing

        lax.fori_loop(0, size // ROWS, turn, 0)

    def pair_copy(j):
        return copy_to(
            lone.at[j], pair.at[c, j], pair_send.at[j], pair_recv.at[j], {"head": sibling}
        )

    def chip_copy(there, i, p):
        j = there * owned + i
        return copy_to(
            chip.at[j, piece(p)], arrived.at[x, i, piece(p)],
            chip_send.at[j, p], chip_recv.at[x, i, p], {"head": there * 2 + c},
        )

    def join_pair(there, i, far):
        j = there * owned + i
        h = (there * 2 + c) * owned + i
        copy_to(
            lone.at[j], pair.at[1 - c, j], pair_send.at[j], pair_recv.at[j], {"head": sibling}
        ).wait_recv()
        fade = jnp.exp(total(x * 2 + 1, h, VALUE_DIM // 128))
        for p in range(PIECES):

            def put(rows):
                joined = (
                    fade * pair[0, j, rows, :].astype(jnp.float32)
                    + pair[1, j, rows, :].astype(jnp.float32)
                ).astype(jnp.bfloat16)
                if far:
                    chip[j, rows, :] = joined
                else:
                    arrived[x, i, rows, :] = joined

            by_piece_rows(p, put)
            if far:
                chip_copy(there, i, p).start()

    def make_states(there, i):
        j = there * owned + i
        lone[j] = chunk_state((there * 2 + (1 - c)) * owned + i)
        pair[c, j] = chunk_state((there * 2 + c) * owned + i)

    def states(there, i):
        j = there * owned + i
        lone[j] = chunk_state((there * 2 + (1 - c)) * owned + i)
        pair_copy(j).start()
        pair[c, j] = chunk_state((there * 2 + c) * owned + i)

    def far_place(t):
        return lax.rem(x + 1 + lax.rem(t, chips - 1), chips), lax.div(t, chips - 1)

    def tot_arrived(source):
        copy_to(
            tots.at[source], tots.at[source], tot_send.at[0], tot_recv.at[source],
            {"head": sibling},
        ).wait_recv()

    loads[1].wait()
    loads[2].wait()
    head_there, head_i = far_place(0)
    make_states(head_there, head_i)
    neighbours = jnp.minimum(block, 1) + jnp.minimum(blocks - 1 - block, 1)
    pl.semaphore_wait(barrier, peers - 1 + neighbours)
    for step in range(1, peers):
        tot_copy(step, me).start()
    pair_copy(head_there * owned + head_i).start()
    loads[3].wait()
    for step in range(1, peers):
        gain_copy(step, me).start()
    tot_arrived(sibling)
    join_pair(head_there, head_i, True)

    def far_states(t, nothing):
        there, i = far_place(t)
        states(there, i)

        @pl.when(t > 1)
        def _():
            before_there, before_i = far_place(t - 1)
            join_pair(before_there, before_i, True)

        return nothing

    far = (chips - 1) * owned
    lax.fori_loop(1, far, far_states, 0)
    states(x, 0)
    if far > 1:
        last_there, last_i = far_place(far - 1)
        join_pair(last_there, last_i, True)
    for load in loads[4:]:
        load.wait()
    for source in range(peers):

        @pl.when(x != source // 2)
        def _():
            tot_arrived(source)

    def inside(h):
        gaps = wcol[h] - wrow[pl.ds(h, 1), :]
        damping = jnp.where(causal, jnp.exp(jnp.where(causal, gaps, 0.0)), 0.0)
        scores = lax.dot_general(
            columns(q_ref, h, KEY_DIM), columns(k_ref, h, KEY_DIM), (((1,), (1,)), ((), ())),
            preferred_element_type=jnp.float32,
        )
        weights = (scores * scale * damping).astype(jnp.bfloat16)
        local[:, pl.ds(pl.multiple_of(h * VALUE_DIM, VALUE_DIM), VALUE_DIM)] = jnp.dot(
            weights, columns(v_ref, h, VALUE_DIM), preferred_element_type=jnp.float32
        )

    def after_copy(i, p):
        return copy_to(
            after.at[i, piece(p)], before.at[i, piece(p)],
            after_send.at[i, p], after_recv.at[i, p], {"ctx": block + 1},
        )

    def carry_copy(there, i, p):
        j = x * owned + i
        return copy_to(
            onward.at[there, i, piece(p)], carry.at[0, j, piece(p)],
            carry_send.at[there, i, p], carry_recv.at[j, p], {"head": there * 2 + c},
        )

    def chain(i, p):
        h = me * owned + i
        for step in range(1, chips):
            there = lax.rem(x + step, chips)
            copy_to(
                chip.at[there * owned + i, piece(p)], arrived.at[there, i, piece(p)],
                chip_send.at[there * owned + i, p], chip_recv.at[there, i, p],
                {"head": there * 2 + c},
            ).wait_recv()

        @pl.when(block > 0)
        def _():
            copy_to(
                after.at[i, piece(p)], before.at[i, piece(p)],
                after_send.at[i, p], after_recv.at[i, p], {"ctx": block - 1},
            ).wait_recv()

        @pl.when(block == 0)
        def _():
            before[i, piece(p)] = jnp.zeros((KEY_DIM // PIECES, VALUE_DIM), jnp.bfloat16)

        fades = [
            jnp.exp(total(2 * n, h, VALUE_DIM // 128) + total(2 * n + 1, h, VALUE_DIM // 128))
            for n in range(chips)
        ]

        def put(rows):
            state = before[i, rows, :].astype(jnp.float32)
            for n in range(chips):
                onward[n, i, rows, :] = state.astype(jnp.bfloat16)
                state = fades[n] * state + arrived[n, i, rows, :].astype(jnp.float32)
            after[i, rows, :] = state.astype(jnp.bfloat16)

        by_piece_rows(p, put)

        @pl.when(block < last)
        def _():
            after_copy(i, p).start()

        for step in range(1, chips):
            carry_copy(lax.rem(x + step, chips), i, p).start()

    def locals_of(i):
        def local_head(n, nothing):
            inside(n * owned + i)
            return nothing

        lax.fori_loop(0, peers, local_head, 0)

    def own_heads(i, nothing):
        @pl.when(block > 0)
        def _():
            locals_of(i)

        join_pair(x, i, False)
        for p in range(PIECES):
            chain(i, p)
        carry[0, x * owned + i] = onward[x, i]

        @pl.when(i < owned - 1)
        def _():
            states(x, i + 1)

        @pl.when(block == 0)
        def _():
            locals_of(i)

        @pl.when(jnp.logical_and(block == last, i > 0))
        def _():
            spread_all(i - 1, 0)

        return nothing

    def out_copy(h):
        place = pl.ds(pl.multiple_of(h * VALUE_DIM, VALUE_DIM), VALUE_DIM)
        return pltpu.make_async_copy(
            out_ref.at[:, place], out_hbm.at[:, place], out_sem.at[h]
        )

    def finish(device, i, state):
        h = device * owned + i
        inter = jnp.dot(columns(q_ref, h, KEY_DIM), state, preferred_element_type=jnp.float32)
        rise = jnp.exp(wcol[h]) * scale
        retained = columns(local, h, VALUE_DIM) + inter * wide(rise, VALUE_DIM // 128)
        centered = retained - jnp.mean(retained, axis=-1, keepdims=True)
        spread = jnp.mean(centered * centered, axis=-1, keepdims=True)
        gain = gains[device, :, pl.ds(pl.multiple_of(i * VALUE_DIM, VALUE_DIM), VALUE_DIM)]
        normed = (centered * lax.rsqrt(spread + 1e-06) * gain).astype(jnp.bfloat16)
        gate = columns(g_ref, h, VALUE_DIM).astype(jnp.float32)
        out_ref[:, pl.ds(pl.multiple_of(h * VALUE_DIM, VALUE_DIM), VALUE_DIM)] = (
            normed.astype(jnp.float32) * (gate / (1.0 + jnp.exp(-gate)))
        ).astype(jnp.bfloat16)
        out_copy(h).start()

    def given_copy(j, p):
        return copy_to(
            carry.at[1 - c, j, piece(p)], given.at[j, piece(p)],
            given_send.at[j, p], given_recv.at[j, p], {"head": sibling},
        )

    def take_given(there, i):
        j = there * owned + i
        for p in range(PIECES):
            given_copy(j, p).wait_recv()
        finish(there * 2 + (1 - c), i, given[j])

    def spread(there, i, far):
        j = there * owned + i
        h = (there * 2 + c) * owned + i
        fade = jnp.exp(total(x * 2, h, VALUE_DIM // 128))
        for p in range(PIECES):
            if far:
                copy_to(
                    onward.at[there, i, piece(p)], carry.at[0, j, piece(p)],
                    carry_send.at[there, i, p], carry_recv.at[j, p], {"head": there * 2 + c},
                ).wait_recv()

            def put(rows):
                carry[1, j, rows, :] = (
                    fade * carry[0, j, rows, :].astype(jnp.float32)
                    + pair[0, j, rows, :].astype(jnp.float32)
                ).astype(jnp.bfloat16)

            by_piece_rows(p, put)
            given_copy(j, p).start()
        finish(there * 2 + c, i, carry[c, j])

    def spread_all(i, nothing):
        spread(x, i, False)
        take_given(x, i)

        def turn(step, nothing):
            there = lax.rem(x + step, chips)
            spread(there, i, True)
            take_given(there, i)
            return nothing

        lax.fori_loop(1, chips, turn, 0)
        return nothing

    for step in range(1, peers):
        gain_copy(step, lax.rem(me + step, peers)).wait_recv()

    lax.fori_loop(0, owned, own_heads, 0)

    lax.fori_loop(jnp.where(block == last, owned - 1, 0), owned, spread_all, 0)

    def written(h, nothing):
        out_copy(h).wait()
        return nothing

    for step in range(1, peers):
        tot_copy(step, me).wait_send()
        gain_copy(step, me).wait_send()

    def sent(j, nothing):
        pair_copy(j).wait_send()
        for p in range(PIECES):
            given_copy(j, p).wait_send()
        return nothing

    lax.fori_loop(0, half, sent, 0)

    def sent_far(i, nothing):
        for step in range(1, chips):
            there = lax.rem(x + step, chips)
            for p in range(PIECES):
                chip_copy(there, i, p).wait_send()
                carry_copy(there, i, p).wait_send()

        @pl.when(block < last)
        def _():
            for p in range(PIECES):
                after_copy(i, p).wait_send()

        return nothing

    lax.fori_loop(0, owned, sent_far, 0)
    lax.fori_loop(0, heads, written, 0)


def rewrite(source, target, stage, sem, out_sem):
    rows = source.shape[0] // PARTS
    parts = [pl.ds(n * rows, rows) for n in range(PARTS)]
    reads = [
        pltpu.make_async_copy(source.at[part], stage.at[part], sem.at[n])
        for n, part in enumerate(parts)
    ]
    writes = [
        pltpu.make_async_copy(stage.at[part], target.at[part], out_sem.at[n])
        for n, part in enumerate(parts)
    ]
    for read in reads:
        read.start()
    for read, write in zip(reads, writes):
        read.wait()
        write.start()
    for write in writes:
        write.wait()


def body(peers, blocks, query_rows, key_rows, value_rows, gate_rows, decay_log, norm_gain):
    tokens, heads = decay_log.shape
    chips, owned, half = peers // 2, heads // peers, heads // 2
    state = (KEY_DIM, VALUE_DIM)
    dma = pltpu.SemaphoreType.DMA
    width = norm_gain.shape[0]
    retained = pl.pallas_call(
        functools.partial(kernel, peers, blocks, heads),
        out_shape=jax.ShapeDtypeStruct(value_rows.shape, jnp.bfloat16),
        in_specs=[pl.BlockSpec(memory_space=pl.ANY)] * 6,
        out_specs=pl.BlockSpec(memory_space=pl.ANY),
        scratch_shapes=[
            pltpu.VMEM(query_rows.shape, jnp.bfloat16),
            pltpu.VMEM(key_rows.shape, jnp.bfloat16),
            pltpu.VMEM(value_rows.shape, jnp.bfloat16),
            pltpu.VMEM(gate_rows.shape, jnp.bfloat16),
            pltpu.VMEM((heads, tokens), jnp.bfloat16),
            pltpu.VMEM(value_rows.shape, jnp.bfloat16),
            dma((6,)), dma((heads,)),
            pltpu.VMEM((peers, heads, 128), jnp.float32),
            pltpu.VMEM((peers, 1, width), jnp.float32),
            pltpu.VMEM((heads, tokens, 128), jnp.float32),
            pltpu.VMEM((heads, tokens), jnp.float32),
            pltpu.VMEM((tokens, heads * VALUE_DIM), jnp.float32),
            pltpu.VMEM((2, half) + state, jnp.bfloat16),
            pltpu.VMEM((half,) + state, jnp.bfloat16),
            pltpu.VMEM((half,) + state, jnp.bfloat16),
            pltpu.VMEM((chips, owned) + state, jnp.bfloat16),
            pltpu.VMEM((owned,) + state, jnp.bfloat16),
            pltpu.VMEM((owned,) + state, jnp.bfloat16),
            pltpu.VMEM((chips, owned) + state, jnp.bfloat16),
            pltpu.VMEM((2, half) + state, jnp.bfloat16),
            pltpu.VMEM((half,) + state, jnp.bfloat16),
            dma((peers,)), dma((peers,)), dma((peers,)), dma((peers,)),
            dma((half,)), dma((half,)),
            dma((half, PIECES)), dma((chips, owned, PIECES)),
            dma((owned, PIECES)), dma((owned, PIECES)),
            dma((chips, owned, PIECES)), dma((half, PIECES)),
            dma((half, PIECES)), dma((half, PIECES)),
        ],
        compiler_params=pltpu.CompilerParams(
            collective_id=0, has_side_effects=True, vmem_limit_bytes=60 * 1024 * 1024
        ),
    )(query_rows, key_rows, value_rows, gate_rows, decay_log.T, norm_gain.reshape(1, width))
    return pl.pallas_call(
        rewrite,
        out_shape=jax.ShapeDtypeStruct(retained.shape, retained.dtype),
        in_specs=[pl.BlockSpec(memory_space=pl.ANY)],
        out_specs=pl.BlockSpec(memory_space=pl.ANY),
        scratch_shapes=[
            pltpu.VMEM(retained.shape, retained.dtype), dma((PARTS,)), dma((PARTS,))
        ],
    )(retained)


def solution(mesh):
    rows = P(("groups", "ctx", "head"), None)
    return jax.shard_map(
        functools.partial(body, mesh.shape["head"], mesh.shape["ctx"]),
        mesh=mesh,
        in_specs=(rows, rows, rows, rows, rows, P("head")),
        out_specs=rows,
        check_vma=False,
    )
```
